32 devices in a mesh: groups: 2 (over x), region: 16 (over z, y, core).
Axes of the slice: x: 2, y: 2, z: 4, core: 2. Of those that a mesh axis runs over, the one named last changes fastest.
Arguments:
- tangent: float32 [4096, 10, 128], P(('groups', 'region')), parts along dimension 0, may hold values from -6 to 6
- transport: bfloat16 [2, 2048, 4, 128, 128], P(None, 'region'), may hold values from -0.25 to 0.25
- block_column: int32 [2, 2048, 4], P(None, 'region'), may hold values from 0 to 2047, as said below
- cell_order: int32 [32, 64], P(None, 'region'), may hold values from 0 to 2047, as said below
- depths: int32 [8192], P('region'), may hold values from 1 to 32, as said below
- rates: float32 [32, 8192], P(None, 'region'), may hold values from 0.1 to 1
- coupling: float32 [10, 10], replicated, may hold values from -2 to 2
- sinking: float32 [10], replicated, may hold values from 0.05 to 0.9
Outputs:
- advanced: float32 [4096, 10, 128], P(('groups', 'region')), parts along dimension 0
The draws below stay inside these ranges and needn't reach their ends.
There are 2 independent parts, one for each index of `groups`. The reference program is written for one: setup_inputs(seed, part) draws one part's arguments, and reference() takes and returns one part's arrays. A program takes and returns all parts, laid end to end along the dimension named above; an argument that names none is the same for every part. Nothing has to cross between parts.
Inputs may be any that keep to these rules, and one draw needn't show every extreme that they name: block_column[s, t, b] names a tile held by the region device of tile t or one of its two neighbours, with wrap around. cell_order is a permutation of all tiles; the column blocks of a region device use exactly that device's tiles. `depths`: each region device holds a column of depth 32.
All inputs are finite; a program needn't handle non-finite values.
Results may differ from the reference program's by a relative error of at most 0.0003.
Values sent between devices are 32-bit elements; how exact they have to be, the bound alone decides.
No kernel may reach another device: no remote copies, remote signals or barrier semaphores. Data moves between devices by JAX's collectives and lax.ppermute only.
A program may use at most 128 MiB of HBM per device.

```python
import math
import jax
import jax.numpy as jnp
from jax import lax

NTR = 10
LEV = 32
NB = 4
TILE_DEV = 128
COL_DEV = 512
TILES = 2048
COLUMNS = 8192


def draw_block_column(key, part):
    key = jax.random.fold_in(key, 11)
    regions = TILES // TILE_DEV
    first, second = jax.random.split(key)
    offset = jax.random.randint(first, (2, TILES, NB), -1, 2)
    inner = jax.random.randint(second, (2, TILES, NB), 0, TILE_DEV)
    home = (jnp.arange(TILES, dtype=jnp.int32) // TILE_DEV)[None, :, None]
    return ((home + offset) % regions * TILE_DEV + inner).astype(jnp.int32)


def draw_cell_order(key, part):
    key = jax.random.fold_in(key, 12)
    regions = TILES // TILE_DEV
    keys = jax.random.split(key, regions)
    perms = jax.vmap(lambda k: jax.random.permutation(k, TILE_DEV))(keys).astype(jnp.int32)
    whole = perms + (jnp.arange(regions, dtype=jnp.int32) * TILE_DEV)[:, None]
    whole = whole.reshape(regions, LEV, TILE_DEV // LEV)
    return jnp.transpose(whole, (1, 0, 2)).reshape(LEV, TILES // LEV).astype(jnp.int32)


def draw_depths(key, part):
    key = jax.random.fold_in(key, 13)
    drawn = jax.random.randint(key, (COLUMNS,), 1, LEV + 1)
    first = jnp.arange(COLUMNS, dtype=jnp.int32) % COL_DEV == 0
    return jnp.where(first, LEV, drawn).astype(jnp.int32)


def shard_levels(key, extent, shards, low, largest):
    def one(dim, blocks):
        steps = jax.random.uniform(jax.random.fold_in(jax.random.fold_in(key, 6), dim), (blocks,), jnp.float32, low / len(shards), largest / len(shards))
        return jnp.repeat(jnp.exp(steps), extent[dim] // blocks).reshape((-1,) + (1,) * (len(extent) - dim - 1))

    factor_of = one(*shards[0])
    for cut in shards[1:]:
        factor_of = factor_of * one(*cut)
    return factor_of


def scatter_about(key, dims, deviation, most, cuts=(), held_as=jnp.bfloat16):
    entries = deviation * jax.random.normal(key, dims, jnp.float32)
    if cuts:
        entries = entries * shard_levels(key, dims, cuts, -0.22, 0.18)
    return jnp.clip(entries, -most, most).astype(held_as)


def setup_inputs(seed: int = 0, part: int = 0) -> dict:
    key_of = jax.random.split(jax.random.key(seed), 9)
    part_splits = jax.random.split(jax.random.fold_in(key_of[8], part), 9)
    return {
        "tangent": scatter_about(part_splits[0], (TILES, NTR, 128), 1.0, 6.0, ((0, 16),), jnp.float32),
        "transport": scatter_about(key_of[1], (2, TILES, NB, 128, 128), (NB * 128) ** -0.5, 0.25, ((1, 16),)),
        "block_column": draw_block_column(jax.random.fold_in(key_of[8], 71), part),
        "cell_order": draw_cell_order(jax.random.fold_in(key_of[8], 71), part),
        "depths": draw_depths(jax.random.fold_in(key_of[8], 71), part),
        "rates": jnp.clip(jnp.exp(math.log(1.0) - 2.3025851 * jax.random.uniform(key_of[5], (LEV, COLUMNS), jnp.float32) ** shard_levels(key_of[5], (LEV, COLUMNS), ((1, 16),), -0.2, 0.2)), 0.1, 1.0),
        "coupling": scatter_about(key_of[6], (NTR, NTR), NTR ** -0.5, 2.0, (), jnp.float32),
        "sinking": jnp.clip(jnp.exp(jax.random.uniform(key_of[7], (NTR,), jnp.float32, math.log(0.05), math.log(0.9))), 0.05, 0.9),
    }


def column_chain(cols, rates, depths, coupling, sinking):
    levels = cols.shape[0]
    level_ids = jnp.arange(levels, dtype=jnp.int32)

    def advance(carry, inputs):
        values, rate_row, level = inputs
        mixed = jnp.einsum("rs,bsw->brw", coupling, values, precision=lax.Precision.HIGHEST,
                           preferred_element_type=jnp.float32)
        result = values + rate_row[:, None, :] * mixed + carry
        result = jnp.where((level < depths)[:, None, :], result, jnp.float32(0.0))
        return sinking[None, :, None] * result, result

    start = jnp.zeros(cols.shape[1:], jnp.float32)
    final, outputs = lax.scan(advance, start, (cols, rates, level_ids))
    return outputs


def reference(tangent, transport, block_column, cell_order, depths, rates, coupling, sinking):
    field = tangent
    tiles = field.shape[0]
    tracers = field.shape[1]
    for step in range(2):
        mats = transport[step].reshape(tiles // TILE_DEV, TILE_DEV, NB, 128, 128)
        picks = block_column[step].reshape(tiles // TILE_DEV, TILE_DEV, NB)

        def apply_block(inputs):
            blocks, index = inputs
            picked = field[index]
            return jnp.einsum("tbij,tbrj->tri", blocks.astype(jnp.float32), picked,
                              precision=lax.Precision.HIGHEST, preferred_element_type=jnp.float32)

        field = lax.map(apply_block, (mats, picks)).reshape(tiles, tracers, 128)
    blocks_all = cell_order.shape[1]
    cols = field[cell_order]
    result = column_chain(cols, rates.reshape(LEV, blocks_all, 128), depths.reshape(blocks_all, 128),
                          coupling, sinking)
    back = jnp.zeros((tiles, tracers, 128), jnp.float32)
    back = back.at[cell_order.reshape(-1)].set(result.reshape(LEV * blocks_all, tracers, 128))
    return back
```

```python
import functools

import jax
import jax.numpy as jnp
from jax import lax
from jax.experimental import pallas as pl
from jax.experimental.pallas import tpu as pltpu
from jax.sharding import PartitionSpec as P

GROUP = 8
ROWS = 16
VMEM_LIMIT = 48 * 1024 * 1024


def split_rows(field, row, tiles):
    x = field[pl.ds(row, ROWS, stride=tiles), :]
    high = x.astype(jnp.bfloat16)
    low = (x - high.astype(jnp.float32)).astype(jnp.bfloat16)
    return jnp.concatenate([high, low], axis=0)


def tile_product(slots, field, blocks, t, tile, tiles, nb):
    xs = [split_rows(field, slots[b, t], tiles) for b in range(nb)]
    ts = [blocks[tile, b] for b in range(nb)]
    acc = lax.dot_general(
        jnp.concatenate(xs, axis=1),
        jnp.concatenate(ts, axis=1),
        (((1,), (1,)), ((), ())),
        preferred_element_type=jnp.float32,
    )
    return acc[:ROWS] + acc[ROWS:]


def load_field(own, near, far, field, sem):
    rows = own.shape[0]
    copies = [
        pltpu.make_async_copy(ref, field.at[pl.ds(i * rows, rows)], sem.at[i])
        for i, ref in enumerate((own, near, far))
    ]
    for copy in copies:
        copy.start()
    return copies


def first_kernel(tiles, nb, ntr, slots, own, near, far, transport, out, field, blocks, fsem, bsem):
    copies = load_field(own, near, far, field, fsem)
    chunks = tiles // GROUP

    def block_copy(c):
        at = pl.ds(c * GROUP, GROUP)
        return pltpu.make_async_copy(transport.at[0, at], blocks.at[at], bsem.at[c])

    for c in range(chunks):
        block_copy(c).start()
    for copy in copies:
        copy.wait()

    def step(c, _):
        block_copy(c).wait()
        for u in range(GROUP):
            t = c * GROUP + u
            v = tile_product(slots, field, blocks, t, t, tiles, nb)
            out[pl.ds(t, ntr, stride=tiles), :] = v[:ntr]
        return 0

    lax.fori_loop(0, chunks, step, 0)


def second_kernel(tiles, nb, ntr, levels, slots, order, own, near, far, rates, depths, mix, sink, transport, out,
                  field, blocks, value, fsem, bsem):
    copies = load_field(own, near, far, field, fsem)
    col_blocks = tiles // levels
    per = GROUP // col_blocks
    steps = tiles // GROUP

    def block_copy(n):
        return pltpu.make_async_copy(transport.at[1, order[n]], blocks.at[n], bsem.at[n])

    ahead = 4

    def start_group(c):
        for u in range(GROUP):
            block_copy(c * GROUP + u).start()

    for c in range(ahead):
        start_group(c)
    for copy in copies:
        copy.wait()

    def products(c):
        for u in range(GROUP):
            block_copy(c * GROUP + u).wait()
        for u in range(GROUP):
            n = c * GROUP + u
            value[lax.rem(c, 2), u] = tile_product(slots, field, blocks, order[n], n, tiles, nb)

    def chain(c, carry):
        carry = list(carry)
        for l in range(per):
            k = c * per + l
            for q in range(col_blocks):
                u = l * col_blocks + q
                v = value[lax.rem(c, 2), u]
                mixed = mix[0] * v[0:1]
                for s in range(1, ntr):
                    mixed = mixed + mix[s] * v[s:s + 1]
                cells = slice(q * 128, (q + 1) * 128)
                rate = rates[k, q:q + 1]
                wet = k < depths[:, cells]
                y = jnp.where(wet, v + rate * mixed + carry[q], jnp.float32(0.0))
                carry[q] = sink[...] * y
                out[pl.ds(order[c * GROUP + u], ntr, stride=tiles), :] = y[:ntr]
        return tuple(carry)

    products(0)

    def step(c, carry):
        @pl.when(c + ahead - 1 < steps)
        def _():
            start_group(c + ahead - 1)

        products(c)
        return chain(c - 1, carry)

    carry = tuple(jnp.zeros((ROWS, 128), jnp.float32) for _ in range(col_blocks))
    carry = lax.fori_loop(1, steps, step, carry)
    chain(steps - 1, carry)


def exchange(rows):
    n = lax.axis_size("region")
    near = [(i, i ^ 1) for i in range(n)]
    far = [(i, (i + 1) % n if i % 2 else (i - 1) % n) for i in range(n)]
    b = lax.ppermute(rows, "region", far)
    a = lax.ppermute(rows, "region", near)
    return a, b


def shards(tangent, transport, block_column, cell_order, depths, rates, coupling, sinking):
    tiles, ntr, cells = tangent.shape
    nb = block_column.shape[2]
    levels = cell_order.shape[0]
    rows = ntr * tiles
    here = lax.axis_index("region")
    planar = jnp.transpose(tangent, (1, 0, 2)).reshape(rows, cells)
    near, far = exchange(planar)

    picks = jnp.transpose(block_column, (0, 2, 1))
    home = picks // tiles
    place = jnp.where(home == here, 0, jnp.where(home == (here ^ 1), 1, 2))
    slots = place * rows + picks % tiles
    order = (cell_order - here * tiles).reshape(-1)
    mix = jnp.pad(coupling.T, ((0, 0), (0, ROWS - ntr)))[:, :, None] * jnp.ones((1, 1, cells), jnp.float32)
    sink = jnp.pad(sinking, (0, ROWS - ntr))[:, None] * jnp.ones((1, cells), jnp.float32)

    smem = pl.BlockSpec(memory_space=pltpu.SMEM)
    vmem = pl.BlockSpec(memory_space=pltpu.VMEM)
    anyw = pl.BlockSpec(memory_space=pl.ANY)
    out_shape = jax.ShapeDtypeStruct((rows, cells), jnp.float32)
    params = pltpu.CompilerParams(vmem_limit_bytes=VMEM_LIMIT)
    field = pltpu.VMEM((3 * rows + (ROWS - ntr) * tiles, cells), jnp.float32)
    blocks = pltpu.VMEM((tiles, nb, cells, cells), jnp.bfloat16)
    flops = 2 * 2 * tiles * nb * cells * cells * ntr

    middle = pl.pallas_call(
        functools.partial(first_kernel, tiles, nb, ntr),
        out_shape=out_shape,
        in_specs=[smem, anyw, anyw, anyw, anyw],
        out_specs=vmem,
        scratch_shapes=[field, blocks, pltpu.SemaphoreType.DMA((3,)), pltpu.SemaphoreType.DMA((tiles // GROUP,))],
        compiler_params=params,
        cost_estimate=pl.CostEstimate(flops=flops, bytes_accessed=transport.size, transcendentals=0),
        name="step_one",
    )(slots[0], planar, near, far, transport)

    near, far = exchange(middle)
    result = pl.pallas_call(
        functools.partial(second_kernel, tiles, nb, ntr, levels),
        out_shape=out_shape,
        in_specs=[smem, smem, anyw, anyw, anyw, vmem, vmem, vmem, vmem, anyw],
        out_specs=vmem,
        scratch_shapes=[
            field,
            blocks,
            pltpu.VMEM((2, GROUP, ROWS, cells), jnp.float32),
            pltpu.SemaphoreType.DMA((3,)),
            pltpu.SemaphoreType.DMA((tiles,)),
        ],
        compiler_params=params,
        cost_estimate=pl.CostEstimate(flops=flops, bytes_accessed=transport.size, transcendentals=0),
        name="step_two_columns",
    )(slots[1], order, middle, near, far, rates.reshape(levels, -1, cells), depths.reshape(1, -1), mix, sink, transport)
    return jnp.transpose(result.reshape(ntr, tiles, cells), (1, 0, 2))


def solution(mesh):
    in_specs = (
        P(("groups", "region"), None, None),
        P(None, "region", None, None, None),
        P(None, "region", None),
        P(None, "region"),
        P("region"),
        P(None, "region"),
        P(),
        P(),
    )
    out_specs = P(("groups", "region"), None, None)
    return jax.shard_map(shards, mesh=mesh, in_specs=in_specs, out_specs=out_specs, check_vma=False)
```

```python
import functools

import jax
import jax.numpy as jnp
from jax import lax
from jax.experimental import pallas as pl
from jax.experimental.pallas import tpu as pltpu
from jax.sharding import PartitionSpec as P

GROUP = 32
CHUNK = 8
LIST = 8
LATE_GROUP = 32
UNROLL = True
DIRECT = 2
SPAN = 4096
NOTHING = 2048
ROWS = 16
VMEM_LIMIT = 12 * 1024 * 1024


def dot_nt(x, t):
    return lax.dot_general(x, t, (((1,), (1,)), ((), ())), preferred_element_type=jnp.float32)


def split_rows(field, row, tiles):
    x = field[pl.ds(row, ROWS, stride=tiles), :]
    high = x.astype(jnp.bfloat16)
    low = (x - high.astype(jnp.float32)).astype(jnp.bfloat16)
    return jnp.concatenate([high, low], axis=0)


def tile_product(slots, field, blocks, t, tiles, nb):
    xs = [split_rows(field, slots[b, t], tiles) for b in range(nb)]
    ts = [blocks[t, b] for b in range(nb)]
    acc = dot_nt(jnp.concatenate(xs, axis=1), jnp.concatenate(ts, axis=1))
    return acc[:ROWS] + acc[ROWS:]


def copy_rows(refs, field, sem):
    copies, row = [], 0
    for i, ref in enumerate(refs):
        copies.append(pltpu.make_async_copy(ref, field.at[pl.ds(row, ref.shape[0])], sem.at[i]))
        row += ref.shape[0]
    for copy in copies:
        copy.start()
    return copies


def block_copy(transport, which, blocks, sem, c):
    at = pl.ds(c * CHUNK, CHUNK)
    return pltpu.make_async_copy(transport.at[which, at], blocks.at[at], sem.at[c])


def prepare_kernel(tiles, ntr, regions, picks_in, order_in, rates_in, coupling_in, sinking, transport,
                   blocks, slots, later_slots, level_rates, mix, sink, picks, order, rates, coupling, sem, ssem):
    chunks = tiles // CHUNK
    small = [pltpu.make_async_copy(src, dst, ssem.at[i]) for i, (src, dst) in enumerate(
        ((picks_in, picks), (order_in, order), (rates_in, rates), (coupling_in, coupling)))]
    for copy in small:
        copy.start()
    for c in range(chunks):
        block_copy(transport, 0, blocks, sem, c).start()
    here = lax.axis_index("region")
    odd = lax.rem(here, 2)
    near = here + 1 - 2 * odd
    far = lax.rem(here + 2 * odd - 1 + regions, regions)
    rows = ntr * tiles
    for copy in small:
        copy.wait()
    nb = picks.shape[1]
    for step, table in enumerate((slots, later_slots)):
        p = picks[step]
        in_here = (p >= here * tiles) & (p < (here + 1) * tiles)
        in_near = (p >= near * tiles) & (p < (near + 1) * tiles)
        table[0:nb, :] = jnp.where(in_here, p - here * tiles,
                                   jnp.where(in_near, p - near * tiles + rows, p - far * tiles + 2 * rows))
    later_slots[nb:, :] = jnp.zeros((later_slots.shape[0] - nb, later_slots.shape[1]), jnp.int32)
    later_slots[nb:nb + order.shape[0], 0:order.shape[1]] = order[...] - here * tiles
    for q in range(level_rates.shape[1]):
        level_rates[:, q, :] = rates[:, q * 128:(q + 1) * 128]
    mix[...] = jnp.zeros_like(mix)
    sink[...] = jnp.zeros_like(sink)
    for s in range(ntr):
        mix[s, 0:ntr, :] = jnp.broadcast_to(coupling[:, s:s + 1], (ntr, 128))
        sink[s:s + 1, :] = jnp.full((1, 128), sinking[s], jnp.float32)
    for c in range(chunks):
        block_copy(transport, 0, blocks, sem, c).wait()


def first_kernel(tiles, nb, ntr, slots, own, near, far, blocks, transport, out, later_blocks, field, fsem, bsem):
    copies = copy_rows((own, near, far), field, fsem)
    chunks = tiles // CHUNK
    for c in range(chunks):
        block_copy(transport, 1, later_blocks, bsem, c).start()
    for copy in copies:
        copy.wait()

    def step(c, _):
        for u in range(GROUP):
            t = c * GROUP + u
            v = tile_product(slots, field, blocks, t, tiles, nb)
            out[pl.ds(t, ntr, stride=tiles), :] = v[:ntr]
        return 0

    lax.fori_loop(0, tiles // GROUP, step, 0)
    for c in range(chunks):
        block_copy(transport, 1, later_blocks, bsem, c).wait()


def early_kernel(tiles, nb, ntr, levels, slots, own, near, near_end, blocks, partial, table, field, fsem):
    copies = copy_rows((own, near, near_end), field, fsem)
    rows = ntr * tiles
    field[2 * rows:, :] = jnp.zeros((field.shape[0] - 2 * rows, 128), jnp.float32)
    for copy in copies:
        copy.wait()
    order_at, count_at, list_at = table_places(tiles, nb)
    col_blocks = tiles // levels

    def step(c, n):
        for u in range(GROUP):
            t = c * GROUP + u
            partial[t] = tile_product(slots, field, blocks, t, tiles, nb)
            used = jnp.int32(0)
            for b in range(nb):
                p = slots[b, t] - 2 * rows
                table[used * tiles + t] = b * SPAN + p
                used = used + (p >= 0).astype(jnp.int32)
            for b in range(DIRECT):
                table[(used + b) * tiles + t] = NOTHING
            for b in range(DIRECT, nb):
                table[list_at + n] = t * (nb * SPAN) + table[b * tiles + t]
                n = n + (used > b).astype(jnp.int32)
        return n

    n = lax.fori_loop(0, tiles // GROUP, step, jnp.int32(0))
    table[count_at] = n
    for i in range(LIST):
        table[list_at + n + i] = NOTHING

    def move(k, _):
        for q in range(col_blocks):
            table[order_at + k * col_blocks + q] = slots[nb + q, k]
        return 0

    lax.fori_loop(0, levels, move, 0)


def table_places(tiles, nb):
    order_at = (nb + DIRECT) * tiles
    count_at = order_at + tiles
    return order_at, count_at, count_at + tiles


def late_kernel(tiles, nb, ntr, levels, table, far, partial, blocks, rates, depths, mix, sink,
                out, field, total, value, fsem, tsem):
    order_at, count_at, list_at = table_places(tiles, nb)
    whole = pltpu.make_async_copy(partial, total, tsem)
    whole.start()
    copies = copy_rows((far,), field, fsem)
    field[NOTHING:, :] = jnp.zeros((field.shape[0] - NOTHING, 128), jnp.float32)
    for copy in copies:
        copy.wait()
    whole.wait()

    def place(e):
        return lax.div(e, SPAN), lax.rem(e, SPAN)

    def rest(i, _):
        found = []
        for u in range(LIST):
            block, row = place(table[list_at + i * LIST + u])
            t = block // nb
            r = dot_nt(split_rows(field, row, tiles), blocks[t, lax.rem(block, nb)])
            found.append((t, r[:ROWS] + r[ROWS:]))
        for t, r in found:
            total[t] += r
        return 0

    lax.fori_loop(0, lax.div(table[count_at] + LIST - 1, LIST), rest, 0)

    col_blocks = tiles // levels
    per = LATE_GROUP // col_blocks
    steps = tiles // LATE_GROUP

    def products(c):
        for u in range(LATE_GROUP):
            t = table[order_at + c * LATE_GROUP + u]
            xs, ts = [], []
            for m in range(DIRECT):
                b, row = place(table[m * tiles + t])
                xs.append(split_rows(field, row, tiles))
                ts.append(blocks[t, b])
            r = dot_nt(jnp.concatenate(xs, axis=1), jnp.concatenate(ts, axis=1))
            value[c % 2 if isinstance(c, int) else lax.rem(c, 2), u] = r[:ROWS] + r[ROWS:] + total[t]

    def chain(c, carry):
        carry = list(carry)
        for l in range(per):
            k = c * per + l
            for q in range(col_blocks):
                u = l * col_blocks + q
                t = table[order_at + c * LATE_GROUP + u]
                v = value[c % 2 if isinstance(c, int) else lax.rem(c, 2), u]
                mixed = mix[0] * v[0:1]
                for s in range(1, ntr):
                    mixed = mixed + mix[s] * v[s:s + 1]
                wet = k < depths[:, q * 128:(q + 1) * 128]
                y = jnp.where(wet, v + rates[k, q:q + 1] * mixed + carry[q], jnp.float32(0.0))
                carry[q] = sink[...] * y
                out[pl.ds(t, ntr, stride=tiles), :] = y[:ntr]
        return tuple(carry)

    carry = tuple(jnp.zeros((ROWS, 128), jnp.float32) for _ in range(col_blocks))
    products(0)

    def step(c, carry):
        products(c)
        return chain(c - 1, carry)

    if UNROLL:
        for c in range(1, steps):
            carry = step(c, carry)
    else:
        carry = lax.fori_loop(1, steps, step, carry)
    chain(steps - 1, carry)


def exchange(rows):
    n = lax.axis_size("region")
    near = [(i, i ^ 1) for i in range(n)]
    far = [(i, (i + 1) % n if i % 2 else (i - 1) % n) for i in range(n)]
    b = lax.ppermute(rows, "region", far)
    a = lax.ppermute(rows, "region", near)
    return a, b


def exchange_split(rows):
    n = lax.axis_size("region")
    near = [(i, i ^ 1) for i in range(n)]
    far = [(i, (i + 1) % n if i % 2 else (i - 1) % n) for i in range(n)]
    b = lax.ppermute(rows, "region", far)
    half = rows.shape[0] // 2
    a = [lax.ppermute(rows[i * half:(i + 1) * half], "region", near) for i in range(2)]
    return a, b


def shards(tangent, transport, block_column, cell_order, depths, rates, coupling, sinking):
    tiles, ntr, cells = tangent.shape
    nb = block_column.shape[2]
    levels, col_blocks = cell_order.shape
    rows = ntr * tiles
    chunks = tiles // CHUNK
    planar = jnp.transpose(tangent, (1, 0, 2)).reshape(rows, cells)
    near, far = exchange(planar)

    smem = pl.BlockSpec(memory_space=pltpu.SMEM)
    vmem = pl.BlockSpec(memory_space=pltpu.VMEM)
    anyw = pl.BlockSpec(memory_space=pl.ANY)
    params = pltpu.CompilerParams(vmem_limit_bytes=VMEM_LIMIT)
    cost = pl.CostEstimate(
        flops=4 * tiles * nb * cells * cells * ntr, bytes_accessed=transport.size, transcendentals=0
    )
    f32, i32 = jnp.float32, jnp.int32
    array = jax.ShapeDtypeStruct
    blocks_shape = pltpu.VMEM(transport.shape[1:], transport.dtype)
    pad = (ROWS - ntr) * tiles
    sems = pltpu.SemaphoreType.DMA

    hbm = pl.BlockSpec(memory_space=pltpu.HBM)
    first_blocks, first_slots, second_slots, level_rates, mix, sink = pl.pallas_call(
        functools.partial(prepare_kernel, tiles, ntr, lax.axis_size("region")),
        out_shape=(
            blocks_shape,
            array((nb, tiles), i32),
            array((nb + max(nb, col_blocks), tiles), i32),
            array((levels, col_blocks, cells), f32),
            array((ntr, ROWS, cells), f32),
            array((ROWS, cells), f32),
        ),
        in_specs=[hbm, hbm, hbm, hbm, smem, anyw],
        out_specs=[vmem] * 6,
        scratch_shapes=[
            pltpu.VMEM((2, nb, tiles), i32),
            pltpu.VMEM((col_blocks, levels), i32),
            pltpu.VMEM(rates.shape, f32),
            pltpu.VMEM(coupling.shape, f32),
            sems((chunks,)),
            sems((4,)),
        ],
        compiler_params=params,
        cost_estimate=cost,
        name="prepare",
    )(jnp.transpose(block_column, (0, 2, 1)), cell_order.T, rates, coupling, sinking, transport)

    middle, second_blocks = pl.pallas_call(
        functools.partial(first_kernel, tiles, nb, ntr),
        out_shape=(array((rows, cells), f32), blocks_shape),
        in_specs=[smem, anyw, anyw, anyw, vmem, anyw],
        out_specs=[vmem, vmem],
        scratch_shapes=[pltpu.VMEM((3 * rows + pad, cells), f32), sems((3,)), sems((chunks,))],
        compiler_params=params,
        cost_estimate=cost,
        name="step_one",
    )(first_slots, pltpu.with_memory_space_constraint(planar, pltpu.VMEM), near, far, first_blocks, transport)

    near, far = exchange_split(middle)
    table_size = table_places(tiles, nb)[2] + (nb - DIRECT) * tiles + LIST
    partial, table = pl.pallas_call(
        functools.partial(early_kernel, tiles, nb, ntr, levels),
        out_shape=(array((tiles, ROWS, cells), f32), array((table_size,), i32)),
        in_specs=[smem, anyw, anyw, anyw, vmem],
        out_specs=[vmem, smem],
        scratch_shapes=[pltpu.VMEM((3 * rows + pad, cells), f32), sems((3,))],
        compiler_params=params,
        cost_estimate=pl.CostEstimate(flops=0, bytes_accessed=0, transcendentals=0),
        name="step_two_early",
    )(second_slots, middle, *near, second_blocks)

    result = pl.pallas_call(
        functools.partial(late_kernel, tiles, nb, ntr, levels),
        out_shape=array((rows, cells), f32),
        in_specs=[smem, anyw] + [vmem] * 6,
        out_specs=vmem,
        scratch_shapes=[
            pltpu.VMEM((2 * NOTHING, cells), f32),
            pltpu.VMEM((tiles, ROWS, cells), f32),
            pltpu.VMEM((2, LATE_GROUP, ROWS, cells), f32),
            sems((1,)),
            sems,
        ],
        compiler_params=params,
        cost_estimate=cost,
        name="step_two_late",
    )(table, far, partial, second_blocks, level_rates, depths.reshape(1, -1), mix, sink)
    return jnp.transpose(result.reshape(ntr, tiles, cells), (1, 0, 2))


def solution(mesh):
    in_specs = (
        P(("groups", "region"), None, None),
        P(None, "region", None, None, None),
        P(None, "region", None),
        P(None, "region"),
        P("region"),
        P(None, "region"),
        P(),
        P(),
    )
    out_specs = P(("groups", "region"), None, None)
    return jax.shard_map(shards, mesh=mesh, in_specs=in_specs, out_specs=out_specs, check_vma=False)
```

```python
import functools

import jax
import jax.numpy as jnp
from jax import lax
from jax.experimental import pallas as pl
from jax.experimental.pallas import tpu as pltpu
from jax.sharding import PartitionSpec as P

GROUP = 16
CHUNK = 8
LIST = 8
LATE_GROUP = 16
UNROLL = True
DIRECT = 2
SPAN = 4096
NOTHING = 2048
ROWS = 16
VMEM_LIMIT = 12 * 1024 * 1024


def dot_nt(x, t):
    return lax.dot_general(x, t, (((1,), (1,)), ((), ())), preferred_element_type=jnp.float32)


def split_rows(field, row, tiles):
    x = field[pl.ds(row, ROWS, stride=tiles), :]
    high = x.astype(jnp.bfloat16)
    low = (x - high.astype(jnp.float32)).astype(jnp.bfloat16)
    return jnp.concatenate([high, low], axis=0)


def copy_rows(refs, field, sem):
    copies, row = [], 0
    for i, ref in enumerate(refs):
        copies.append(pltpu.make_async_copy(ref, field.at[pl.ds(row, ref.shape[0])], sem.at[i]))
        row += ref.shape[0]
    for copy in copies:
        copy.start()
    return copies


def block_copy(transport, which, blocks, sem, c):
    at = pl.ds(c * CHUNK, CHUNK)
    return pltpu.make_async_copy(transport.at[which, at], blocks.at[at], sem.at[c])


def split_index(index, size):
    if size & (size - 1) == 0:
        high = lax.shift_right_logical(index, jnp.int32(size.bit_length() - 1))
    else:
        high = lax.div(index, jnp.int32(size))
    return high, index - high * size


def table_rows(nb, col_blocks):
    order_row = 2 * nb
    list_row = order_row + col_blocks
    return order_row, list_row, list_row + nb


def index_table(tiles, nb, ntr, regions, picks, staged):
    here = lax.axis_index("region")
    odd = lax.rem(here, 2)
    near = here + 1 - 2 * odd
    far = lax.rem(here + 2 * odd - 1 + regions, regions)
    rows = ntr * tiles
    staged[...] = jnp.zeros_like(staged)
    chosen = [jnp.full((1, tiles), NOTHING, jnp.int32) for _ in range(nb)]
    used = jnp.zeros((1, tiles), jnp.int32)
    for b in range(nb):
        p = picks[b:b + 1, :]
        in_here = (p >= here * tiles) & (p < (here + 1) * tiles)
        in_near = (p >= near * tiles) & (p < (near + 1) * tiles)
        distant = jnp.where(in_here | in_near, 0, 1)
        away = p - far * tiles
        staged[b:b + 1, :] = jnp.where(in_here, p - here * tiles, jnp.where(in_near, p - near * tiles + rows, 2 * rows))
        for m in range(b + 1):
            chosen[m] = jnp.where((distant == 1) & (used == m), away + b * SPAN, chosen[m])
        used = used + distant
    for m in range(nb):
        staged[nb + m:nb + m + 1, :] = chosen[m]
    return here


def early_products(tiles, nb, col_blocks, table, field, blocks, partial, ready):
    order_row, list_row, count_row = table_rows(nb, col_blocks)

    def put(n, e):
        row, lane = split_index(n, tiles)
        table[list_row + row, lane] = e

    def step(c, n):
        ready(c)
        for u in range(GROUP):
            t = c * GROUP + u
            xs = [split_rows(field, table[b, t], tiles) for b in range(nb)]
            for m in range(DIRECT, nb):
                e = table[nb + m, t]
                put(n, t * (nb * SPAN) + e)
                n = n + jnp.where(e == NOTHING, 0, 1).astype(jnp.int32)
            r = dot_nt(jnp.concatenate(xs, axis=1), jnp.concatenate([blocks[t, b] for b in range(nb)], axis=1))
            partial[t] = r[:ROWS] + r[ROWS:]
        return n

    n = lax.fori_loop(0, tiles // GROUP, step, jnp.int32(0))
    table[count_row, 0] = n
    for i in range(LIST):
        put(n + i, NOTHING)


def early_first_kernel(tiles, nb, ntr, col_blocks, regions, picks_in, own, near, transport, blocks, partial, table,
                       picks, staged, field, psem, fsem, bsem):
    index = pltpu.make_async_copy(picks_in.at[0], picks, psem)
    index.start()
    copies = copy_rows((own, near), field, fsem)
    for c in range(tiles // CHUNK):
        block_copy(transport, 0, blocks, bsem, c).start()
    rows = ntr * tiles
    field[2 * rows:, :] = jnp.zeros((field.shape[0] - 2 * rows, 128), jnp.float32)
    index.wait()
    index_table(tiles, nb, ntr, regions, picks, staged)
    index = pltpu.make_async_copy(staged, table, psem)
    index.start()
    for copy in copies:
        copy.wait()
    index.wait()

    def ready(c):
        for i in range(GROUP // CHUNK):
            block_copy(transport, 0, blocks, bsem, c * (GROUP // CHUNK) + i).wait()

    early_products(tiles, nb, col_blocks, table, field, blocks, partial, ready)


def early_second_kernel(tiles, nb, ntr, col_blocks, regions, picks_in, order_in, rates_in, coupling_in, sinking,
                        own, near, near_end, transport, blocks, partial, table, level_rates, mix, sink,
                        picks, staged, field, order, rates, coupling, psem, fsem, ssem, bsem):
    index = pltpu.make_async_copy(picks_in.at[1], picks, psem)
    index.start()
    small = [pltpu.make_async_copy(src, dst, ssem.at[i]) for i, (src, dst) in enumerate(
        ((order_in, order), (rates_in, rates), (coupling_in, coupling)))]
    for copy in small:
        copy.start()
    copies = copy_rows((own, near, near_end), field, fsem)
    for c in range(tiles // CHUNK):
        block_copy(transport, 1, blocks, bsem, c).start()
    rows = ntr * tiles
    field[2 * rows:, :] = jnp.zeros((field.shape[0] - 2 * rows, 128), jnp.float32)
    index.wait()
    for copy in small:
        copy.wait()
    here = index_table(tiles, nb, ntr, regions, picks, staged)
    order_row = table_rows(nb, col_blocks)[0]
    staged[order_row:order_row + col_blocks, 0:order.shape[1]] = order[...] - here * tiles
    index = pltpu.make_async_copy(staged, table, psem)
    index.start()
    for q in range(col_blocks):
        level_rates[:, q, :] = rates[:, q * 128:(q + 1) * 128]
    mix[...] = jnp.zeros_like(mix)
    sink[...] = jnp.zeros_like(sink)
    for s in range(ntr):
        mix[s, 0:ntr, :] = jnp.broadcast_to(coupling[:, s:s + 1], (ntr, 128))
        sink[s:s + 1, :] = jnp.full((1, 128), sinking[s], jnp.float32)
    for copy in copies:
        copy.wait()
    index.wait()

    def ready(c):
        for i in range(GROUP // CHUNK):
            block_copy(transport, 1, blocks, bsem, c * (GROUP // CHUNK) + i).wait()

    early_products(tiles, nb, col_blocks, table, field, blocks, partial, ready)


def place(e):
    return split_index(e, SPAN)


def far_product(tiles, nb, table, field, blocks, t):
    xs, ts = [], []
    for m in range(DIRECT):
        b, row = place(table[nb + m, t])
        xs.append(split_rows(field, row, tiles))
        ts.append(blocks[t, b])
    r = dot_nt(jnp.concatenate(xs, axis=1), jnp.concatenate(ts, axis=1))
    return r[:ROWS] + r[ROWS:]


def load_far(tiles, nb, col_blocks, table, far, blocks, field, total, fsem):
    order_row, list_row, count_row = table_rows(nb, col_blocks)
    copies = copy_rows((far,), field, fsem)
    total[...] = jnp.zeros_like(total)
    field[NOTHING:, :] = jnp.zeros((field.shape[0] - NOTHING, 128), jnp.float32)
    for copy in copies:
        copy.wait()

    def rest(i, _):
        found = []
        for u in range(LIST):
            at, lane = split_index(i * LIST + u, tiles)
            block, row = place(table[list_row + at, lane])
            t, b = split_index(block, nb)
            r = dot_nt(split_rows(field, row, tiles), blocks[t, b])
            found.append((t, r[:ROWS] + r[ROWS:]))
        for t, r in found:
            total[t] += r
        return 0

    lax.fori_loop(0, lax.div(table[count_row, 0] + LIST - 1, LIST), rest, 0)


def late_first_kernel(tiles, nb, ntr, col_blocks, table, far, partial, blocks, out, field, total, fsem):
    load_far(tiles, nb, col_blocks, table, far, blocks, field, total, fsem)
    for t in range(tiles):
        v = far_product(tiles, nb, table, field, blocks, t) + partial[t] + total[t]
        out[pl.ds(t, ntr, stride=tiles), :] = v[:ntr]


def late_second_kernel(tiles, nb, ntr, col_blocks, table, far, partial, blocks, rates, depths, mix, sink,
                       out, field, total, value, fsem):
    load_far(tiles, nb, col_blocks, table, far, blocks, field, total, fsem)
    order_row = table_rows(nb, col_blocks)[0]
    per = LATE_GROUP // col_blocks
    steps = tiles // LATE_GROUP

    def products(c):
        for u in range(LATE_GROUP):
            t = table[order_row + u % col_blocks, c * per + u // col_blocks]
            value[c % 2 if isinstance(c, int) else lax.rem(c, 2), u] = (
                far_product(tiles, nb, table, field, blocks, t) + partial[t] + total[t])

    def chain(c, carry):
        carry = list(carry)
        for l in range(per):
            k = c * per + l
            for q in range(col_blocks):
                u = l * col_blocks + q
                t = table[order_row + q, k]
                v = value[c % 2 if isinstance(c, int) else lax.rem(c, 2), u]
                mixed = mix[0] * v[0:1]
                for s in range(1, ntr):
                    mixed = mixed + mix[s] * v[s:s + 1]
                wet = k < depths[:, q * 128:(q + 1) * 128]
                y = jnp.where(wet, v + rates[k, q:q + 1] * mixed + carry[q], jnp.float32(0.0))
                carry[q] = sink[...] * y
                out[pl.ds(t, ntr, stride=tiles), :] = y[:ntr]
        return tuple(carry)

    carry = tuple(jnp.zeros((ROWS, 128), jnp.float32) for _ in range(col_blocks))
    products(0)

    def step(c, carry):
        products(c)
        return chain(c - 1, carry)

    if UNROLL:
        for c in range(1, steps):
            carry = step(c, carry)
    else:
        carry = lax.fori_loop(1, steps, step, carry)
    chain(steps - 1, carry)


def in_hbm(x):
    return pltpu.with_memory_space_constraint(x, pltpu.HBM)


def exchange(rows):
    n = lax.axis_size("region")
    near = [(i, i ^ 1) for i in range(n)]
    far = [(i, (i + 1) % n if i % 2 else (i - 1) % n) for i in range(n)]
    b = lax.ppermute(rows, "region", far)
    a = lax.ppermute(rows, "region", near)
    return a, b


def exchange_split(rows):
    n = lax.axis_size("region")
    near = [(i, i ^ 1) for i in range(n)]
    far = [(i, (i + 1) % n if i % 2 else (i - 1) % n) for i in range(n)]
    b = lax.ppermute(rows, "region", far)
    half = rows.shape[0] // 2
    a = [lax.ppermute(rows[i * half:(i + 1) * half], "region", near) for i in range(2)]
    return a, b


def shards(tangent, transport, block_column, cell_order, depths, rates, coupling, sinking):
    tiles, ntr, cells = tangent.shape
    nb = block_column.shape[2]
    levels, col_blocks = cell_order.shape
    rows = ntr * tiles
    chunks = tiles // CHUNK
    planar = jnp.transpose(tangent, (1, 0, 2)).reshape(rows, cells)
    near, far = exchange(planar)

    smem = pl.BlockSpec(memory_space=pltpu.SMEM)
    vmem = pl.BlockSpec(memory_space=pltpu.VMEM)
    anyw = pl.BlockSpec(memory_space=pl.ANY)
    params = pltpu.CompilerParams(vmem_limit_bytes=VMEM_LIMIT)
    cost = pl.CostEstimate(
        flops=4 * tiles * nb * cells * cells * ntr, bytes_accessed=transport.size, transcendentals=0
    )
    none = pl.CostEstimate(flops=0, bytes_accessed=0, transcendentals=0)
    f32, i32 = jnp.float32, jnp.int32
    array = jax.ShapeDtypeStruct
    blocks_shape = pltpu.VMEM(transport.shape[1:], transport.dtype)
    pad = (ROWS - ntr) * tiles
    sems = pltpu.SemaphoreType.DMA

    picks = in_hbm(jnp.transpose(block_column, (0, 2, 1)))
    own = in_hbm(planar)
    table_shape = array((table_rows(nb, col_blocks)[2] + 8 & ~7, tiles), i32)
    regions = lax.axis_size("region")
    partial_shape = array((tiles, ROWS, cells), f32)
    picks_scratch = pltpu.VMEM((nb, tiles), i32)
    staged = pltpu.VMEM(table_shape.shape, i32)
    field = pltpu.VMEM((3 * rows + pad, cells), f32)
    far_field = pltpu.VMEM((2 * NOTHING, cells), f32)
    total = pltpu.VMEM((tiles, ROWS, cells), f32)

    blocks, partial, table = pl.pallas_call(
        functools.partial(early_first_kernel, tiles, nb, ntr, col_blocks, regions),
        out_shape=(blocks_shape, partial_shape, table_shape),
        in_specs=[anyw] * 4,
        out_specs=[vmem, vmem, smem],
        scratch_shapes=[picks_scratch, staged, field, sems, sems((2,)), sems((chunks,))],
        compiler_params=params,
        cost_estimate=none,
        name="step_one_early",
    )(picks, own, near, transport)

    middle = pl.pallas_call(
        functools.partial(late_first_kernel, tiles, nb, ntr, col_blocks),
        out_shape=array((rows, cells), f32),
        in_specs=[smem, anyw, vmem, vmem],
        out_specs=vmem,
        scratch_shapes=[far_field, total, sems((1,))],
        compiler_params=params,
        cost_estimate=cost,
        name="step_one_late",
    )(table, far, partial, blocks)

    near, far = exchange_split(middle)
    blocks, partial, table, level_rates, mix, sink = pl.pallas_call(
        functools.partial(early_second_kernel, tiles, nb, ntr, col_blocks, regions),
        out_shape=(
            blocks_shape,
            partial_shape,
            table_shape,
            array((levels, col_blocks, cells), f32),
            array((ntr, ROWS, cells), f32),
            array((ROWS, cells), f32),
        ),
        in_specs=[anyw] * 4 + [smem] + [anyw] * 4,
        out_specs=[vmem, vmem, smem, vmem, vmem, vmem],
        scratch_shapes=[
            picks_scratch,
            staged,
            field,
            pltpu.VMEM((col_blocks, levels), i32),
            pltpu.VMEM(rates.shape, f32),
            pltpu.VMEM(coupling.shape, f32),
            sems,
            sems((3,)),
            sems((3,)),
            sems((chunks,)),
        ],
        compiler_params=params,
        cost_estimate=none,
        name="step_two_early",
    )(picks, in_hbm(cell_order.T), in_hbm(rates), in_hbm(coupling), sinking, middle, *near, transport)

    result = pl.pallas_call(
        functools.partial(late_second_kernel, tiles, nb, ntr, col_blocks),
        out_shape=array((rows, cells), f32),
        in_specs=[smem, anyw] + [vmem] * 6,
        out_specs=vmem,
        scratch_shapes=[far_field, total, pltpu.VMEM((2, LATE_GROUP, ROWS, cells), f32), sems((1,))],
        compiler_params=params,
        cost_estimate=cost,
        name="step_two_late",
    )(table, far, partial, blocks, level_rates, depths.reshape(1, -1), mix, sink)
    return jnp.transpose(result.reshape(ntr, tiles, cells), (1, 0, 2))


def solution(mesh):
    in_specs = (
        P(("groups", "region"), None, None),
        P(None, "region", None, None, None),
        P(None, "region", None),
        P(None, "region"),
        P("region"),
        P(None, "region"),
        P(),
        P(),
    )
    out_specs = P(("groups", "region"), None, None)
    return jax.shard_map(shards, mesh=mesh, in_specs=in_specs, out_specs=out_specs, check_vma=False)
```

```python
import functools

import jax
import jax.numpy as jnp
from jax import lax
from jax.experimental import pallas as pl
from jax.experimental.pallas import tpu as pltpu
from jax.sharding import PartitionSpec as P

GROUP = 16
CHUNK = 8
LIST = 8
STATIC = 24
LATE_GROUP = 16
UNROLL = True
DIRECT = 2
SPAN = 4096
NOTHING = 2048
ROWS = 16
VMEM_LIMIT = 12 * 1024 * 1024


def far_rows(far, row, tiles):
    ntr = far.shape[0] // tiles
    keep = jnp.where(row < tiles, 1.0, 0.0).astype(jnp.float32)
    x = far[pl.ds(jnp.where(row < tiles, row, 0), ntr, stride=tiles), :] * keep
    x = jnp.concatenate([x, jnp.zeros((ROWS - ntr, 128), jnp.float32)], axis=0)
    high = x.astype(jnp.bfloat16)
    low = (x - high.astype(jnp.float32)).astype(jnp.bfloat16)
    return jnp.concatenate([high, low], axis=0)


def dot_nt(x, t):
    return lax.dot_general(x, t, (((1,), (1,)), ((), ())), preferred_element_type=jnp.float32)


def split_rows(field, row, tiles):
    x = field[pl.ds(row, ROWS, stride=tiles), :]
    high = x.astype(jnp.bfloat16)
    low = (x - high.astype(jnp.float32)).astype(jnp.bfloat16)
    return jnp.concatenate([high, low], axis=0)


def copy_rows(refs, field, sem):
    copies, row = [], 0
    for i, ref in enumerate(refs):
        copies.append(pltpu.make_async_copy(ref, field.at[pl.ds(row, ref.shape[0])], sem.at[i]))
        row += ref.shape[0]
    for copy in copies:
        copy.start()
    return copies


def block_copy(transport, which, blocks, sem, c):
    at = pl.ds(c * CHUNK, CHUNK)
    return pltpu.make_async_copy(transport.at[which, at], blocks.at[at], sem.at[c])


def split_index(index, size):
    if size & (size - 1) == 0:
        high = lax.shift_right_logical(index, jnp.int32(size.bit_length() - 1))
    else:
        high = lax.div(index, jnp.int32(size))
    return high, index - high * size


def table_rows(nb, col_blocks):
    order_row = 2 * nb
    list_row = order_row + col_blocks
    return order_row, list_row, list_row + nb


def index_table(tiles, nb, ntr, regions, picks, staged):
    here = lax.axis_index("region")
    odd = lax.rem(here, 2)
    near = here + 1 - 2 * odd
    far = lax.rem(here + 2 * odd - 1 + regions, regions)
    rows = ntr * tiles
    staged[...] = jnp.zeros_like(staged)
    chosen = [jnp.full((1, tiles), NOTHING, jnp.int32) for _ in range(nb)]
    used = jnp.zeros((1, tiles), jnp.int32)
    for b in range(nb):
        p = picks[b:b + 1, :]
        in_here = (p >= here * tiles) & (p < (here + 1) * tiles)
        in_near = (p >= near * tiles) & (p < (near + 1) * tiles)
        distant = jnp.where(in_here | in_near, 0, 1)
        away = p - far * tiles
        staged[b:b + 1, :] = jnp.where(in_here, p - here * tiles, jnp.where(in_near, p - near * tiles + rows, 2 * rows))
        for m in range(b + 1):
            chosen[m] = jnp.where((distant == 1) & (used == m), away + b * SPAN, chosen[m])
        used = used + distant
    for m in range(nb):
        staged[nb + m:nb + m + 1, :] = chosen[m]
    return here


def early_products(tiles, nb, col_blocks, table, field, blocks, partial, ready):
    order_row, list_row, count_row = table_rows(nb, col_blocks)

    def put(n, e):
        row, lane = split_index(n, tiles)
        table[list_row + row, lane] = e

    def step(c, n):
        ready(c)
        for u in range(GROUP):
            t = c * GROUP + u
            xs = [split_rows(field, table[b, t], tiles) for b in range(nb)]
            for m in range(DIRECT, nb):
                e = table[nb + m, t]
                put(n, t * (nb * SPAN) + e)
                n = n + jnp.where(e == NOTHING, 0, 1).astype(jnp.int32)
            r = dot_nt(jnp.concatenate(xs, axis=1), jnp.concatenate([blocks[t, b] for b in range(nb)], axis=1))
            partial[t] = r[:ROWS] + r[ROWS:]
        return n

    n = lax.fori_loop(0, tiles // GROUP, step, jnp.int32(0))
    table[count_row, 0] = n
    for i in range(STATIC):
        put(n + i, NOTHING)


def early_first_kernel(tiles, nb, ntr, col_blocks, regions, picks_in, own, near, transport, blocks, partial, table,
                       picks, staged, field, psem, fsem, bsem):
    index = pltpu.make_async_copy(picks_in.at[0], picks, psem)
    index.start()
    copies = copy_rows((own, near), field, fsem)
    for c in range(tiles // CHUNK):
        block_copy(transport, 0, blocks, bsem, c).start()
    rows = ntr * tiles
    field[2 * rows:, :] = jnp.zeros((field.shape[0] - 2 * rows, 128), jnp.float32)
    index.wait()
    index_table(tiles, nb, ntr, regions, picks, staged)
    index = pltpu.make_async_copy(staged, table, psem)
    index.start()
    for copy in copies:
        copy.wait()
    index.wait()

    def ready(c):
        for i in range(GROUP // CHUNK):
            block_copy(transport, 0, blocks, bsem, c * (GROUP // CHUNK) + i).wait()

    early_products(tiles, nb, col_blocks, table, field, blocks, partial, ready)


def early_second_kernel(tiles, nb, ntr, col_blocks, regions, picks_in, order_in, rates_in, coupling_in, sinking,
                        own, near, near_end, transport, blocks, partial, table, level_rates, mix, sink,
                        picks, staged, field, order, rates, coupling, psem, fsem, ssem, bsem):
    index = pltpu.make_async_copy(picks_in.at[1], picks, psem)
    index.start()
    small = [pltpu.make_async_copy(src, dst, ssem.at[i]) for i, (src, dst) in enumerate(
        ((order_in, order), (rates_in, rates), (coupling_in, coupling)))]
    for copy in small:
        copy.start()
    copies = copy_rows((own, near, near_end), field, fsem)
    for c in range(tiles // CHUNK):
        block_copy(transport, 1, blocks, bsem, c).start()
    rows = ntr * tiles
    field[2 * rows:, :] = jnp.zeros((field.shape[0] - 2 * rows, 128), jnp.float32)
    index.wait()
    for copy in small:
        copy.wait()
    here = index_table(tiles, nb, ntr, regions, picks, staged)
    order_row = table_rows(nb, col_blocks)[0]
    staged[order_row:order_row + col_blocks, 0:order.shape[1]] = order[...] - here * tiles
    index = pltpu.make_async_copy(staged, table, psem)
    index.start()
    for q in range(col_blocks):
        level_rates[:, q, :] = rates[:, q * 128:(q + 1) * 128]
    mix[...] = jnp.zeros_like(mix)
    sink[...] = jnp.zeros_like(sink)
    for s in range(ntr):
        mix[s, 0:ntr, :] = jnp.broadcast_to(coupling[:, s:s + 1], (ntr, 128))
        sink[s:s + 1, :] = jnp.full((1, 128), sinking[s], jnp.float32)
    for copy in copies:
        copy.wait()
    index.wait()

    def ready(c):
        for i in range(GROUP // CHUNK):
            block_copy(transport, 1, blocks, bsem, c * (GROUP // CHUNK) + i).wait()

    early_products(tiles, nb, col_blocks, table, field, blocks, partial, ready)


def place(e):
    return split_index(e, SPAN)


def far_product(tiles, nb, table, field, blocks, t):
    xs, ts = [], []
    for m in range(DIRECT):
        b, row = place(table[nb + m, t])
        xs.append(far_rows(field, row, tiles))
        ts.append(blocks[t, b])
    r = dot_nt(jnp.concatenate(xs, axis=1), jnp.concatenate(ts, axis=1))
    return r[:ROWS] + r[ROWS:]


def load_far(tiles, nb, col_blocks, table, field, blocks, total):
    order_row, list_row, count_row = table_rows(nb, col_blocks)
    total[...] = jnp.zeros_like(total)

    def rest(first, size):
        found = []
        for u in range(size):
            at, lane = split_index(first + u, tiles)
            block, row = place(table[list_row + at, lane])
            t, b = split_index(block, nb)
            r = dot_nt(far_rows(field, row, tiles), blocks[t, b])
            found.append((t, r[:ROWS] + r[ROWS:]))
        for t, r in found:
            total[t] += r

    def more(i, _):
        rest(STATIC + i * LIST, LIST)
        return 0

    lax.fori_loop(0, lax.div(jnp.maximum(table[count_row, 0] - STATIC, 0) + LIST - 1, LIST), more, 0)
    rest(jnp.int32(0), STATIC)


def late_first_kernel(tiles, nb, ntr, col_blocks, table, field, partial, blocks, out, total):
    load_far(tiles, nb, col_blocks, table, field, blocks, total)
    for t in range(tiles):
        v = far_product(tiles, nb, table, field, blocks, t) + partial[t] + total[t]
        out[pl.ds(t, ntr, stride=tiles), :] = v[:ntr]


def late_second_kernel(tiles, nb, ntr, col_blocks, table, field, partial, blocks, rates, depths, mix, sink,
                       out, total, value):
    load_far(tiles, nb, col_blocks, table, field, blocks, total)
    order_row = table_rows(nb, col_blocks)[0]
    per = LATE_GROUP // col_blocks
    steps = tiles // LATE_GROUP

    def products(c):
        for u in range(LATE_GROUP):
            t = table[order_row + u % col_blocks, c * per + u // col_blocks]
            value[c % 2 if isinstance(c, int) else lax.rem(c, 2), u] = (
                far_product(tiles, nb, table, field, blocks, t) + partial[t] + total[t])

    def chain(c, carry):
        carry = list(carry)
        for l in range(per):
            k = c * per + l
            for q in range(col_blocks):
                u = l * col_blocks + q
                t = table[order_row + q, k]
                v = value[c % 2 if isinstance(c, int) else lax.rem(c, 2), u]
                mixed = mix[0] * v[0:1]
                for s in range(1, ntr):
                    mixed = mixed + mix[s] * v[s:s + 1]
                wet = k < depths[:, q * 128:(q + 1) * 128]
                y = jnp.where(wet, v + rates[k, q:q + 1] * mixed + carry[q], jnp.float32(0.0))
                carry[q] = sink[...] * y
                out[pl.ds(t, ntr, stride=tiles), :] = y[:ntr]
        return tuple(carry)

    carry = tuple(jnp.zeros((ROWS, 128), jnp.float32) for _ in range(col_blocks))
    products(0)

    def step(c, carry):
        products(c)
        return chain(c - 1, carry)

    if UNROLL:
        for c in range(1, steps):
            carry = step(c, carry)
    else:
        carry = lax.fori_loop(1, steps, step, carry)
    chain(steps - 1, carry)


def in_hbm(x):
    return pltpu.with_memory_space_constraint(x, pltpu.HBM)


def exchange(rows):
    n = lax.axis_size("region")
    near = [(i, i ^ 1) for i in range(n)]
    far = [(i, (i + 1) % n if i % 2 else (i - 1) % n) for i in range(n)]
    b = lax.ppermute(rows, "region", far)
    a = lax.ppermute(rows, "region", near)
    return a, b


def exchange_split(rows):
    n = lax.axis_size("region")
    near = [(i, i ^ 1) for i in range(n)]
    far = [(i, (i + 1) % n if i % 2 else (i - 1) % n) for i in range(n)]
    b = lax.ppermute(rows, "region", far)
    half = rows.shape[0] // 2
    a = [lax.ppermute(rows[i * half:(i + 1) * half], "region", near) for i in range(2)]
    return a, b


def shards(tangent, transport, block_column, cell_order, depths, rates, coupling, sinking):
    tiles, ntr, cells = tangent.shape
    nb = block_column.shape[2]
    levels, col_blocks = cell_order.shape
    rows = ntr * tiles
    chunks = tiles // CHUNK
    planar = jnp.transpose(tangent, (1, 0, 2)).reshape(rows, cells)
    near, far = exchange(planar)

    smem = pl.BlockSpec(memory_space=pltpu.SMEM)
    vmem = pl.BlockSpec(memory_space=pltpu.VMEM)
    anyw = pl.BlockSpec(memory_space=pl.ANY)
    params = pltpu.CompilerParams(vmem_limit_bytes=VMEM_LIMIT)
    cost = pl.CostEstimate(
        flops=4 * tiles * nb * cells * cells * ntr, bytes_accessed=transport.size, transcendentals=0
    )
    none = pl.CostEstimate(flops=0, bytes_accessed=0, transcendentals=0)
    f32, i32 = jnp.float32, jnp.int32
    array = jax.ShapeDtypeStruct
    blocks_shape = pltpu.VMEM(transport.shape[1:], transport.dtype)
    pad = (ROWS - ntr) * tiles
    sems = pltpu.SemaphoreType.DMA

    picks = in_hbm(jnp.transpose(block_column, (0, 2, 1)))
    own = in_hbm(planar)
    table_shape = array((table_rows(nb, col_blocks)[2] + 8 & ~7, tiles), i32)
    regions = lax.axis_size("region")
    partial_shape = array((tiles, ROWS, cells), f32)
    picks_scratch = pltpu.VMEM((nb, tiles), i32)
    staged = pltpu.VMEM(table_shape.shape, i32)
    field = pltpu.VMEM((3 * rows + pad, cells), f32)
    total = pltpu.VMEM((tiles, ROWS, cells), f32)

    blocks, partial, table = pl.pallas_call(
        functools.partial(early_first_kernel, tiles, nb, ntr, col_blocks, regions),
        out_shape=(blocks_shape, partial_shape, table_shape),
        in_specs=[anyw] * 4,
        out_specs=[vmem, vmem, smem],
        scratch_shapes=[picks_scratch, staged, field, sems, sems((2,)), sems((chunks,))],
        compiler_params=params,
        cost_estimate=none,
        name="step_one_early",
    )(picks, own, near, transport)

    middle = pl.pallas_call(
        functools.partial(late_first_kernel, tiles, nb, ntr, col_blocks),
        out_shape=array((rows, cells), f32),
        in_specs=[smem, vmem, vmem, vmem],
        out_specs=vmem,
        scratch_shapes=[total],
        compiler_params=params,
        cost_estimate=cost,
        name="step_one_late",
    )(table, far, partial, blocks)

    near, far = exchange_split(middle)
    blocks, partial, table, level_rates, mix, sink = pl.pallas_call(
        functools.partial(early_second_kernel, tiles, nb, ntr, col_blocks, regions),
        out_shape=(
            blocks_shape,
            partial_shape,
            table_shape,
            array((levels, col_blocks, cells), f32),
            array((ntr, ROWS, cells), f32),
            array((ROWS, cells), f32),
        ),
        in_specs=[anyw] * 4 + [smem] + [anyw] * 4,
        out_specs=[vmem, vmem, smem, vmem, vmem, vmem],
        scratch_shapes=[
            picks_scratch,
            staged,
            field,
            pltpu.VMEM((col_blocks, levels), i32),
            pltpu.VMEM(rates.shape, f32),
            pltpu.VMEM(coupling.shape, f32),
            sems,
            sems((3,)),
            sems((3,)),
            sems((chunks,)),
        ],
        compiler_params=params,
        cost_estimate=none,
        name="step_two_early",
    )(picks, in_hbm(cell_order.T), in_hbm(rates), in_hbm(coupling), sinking, middle, *near, transport)

    result = pl.pallas_call(
        functools.partial(late_second_kernel, tiles, nb, ntr, col_blocks),
        out_shape=array((rows, cells), f32),
        in_specs=[smem, vmem] + [vmem] * 6,
        out_specs=vmem,
        scratch_shapes=[total, pltpu.VMEM((2, LATE_GROUP, ROWS, cells), f32)],
        compiler_params=params,
        cost_estimate=cost,
        name="step_two_late",
    )(table, far, partial, blocks, level_rates, depths.reshape(1, -1), mix, sink)
    return jnp.transpose(result.reshape(ntr, tiles, cells), (1, 0, 2))


def solution(mesh):
    in_specs = (
        P(("groups", "region"), None, None),
        P(None, "region", None, None, None),
        P(None, "region", None),
        P(None, "region"),
        P("region"),
        P(None, "region"),
        P(),
        P(),
    )
    out_specs = P(("groups", "region"), None, None)
    return jax.shard_map(shards, mesh=mesh, in_specs=in_specs, out_specs=out_specs, check_vma=False)
```

```python
import functools

import jax
import jax.numpy as jnp
from jax import lax
from jax.experimental import pallas as pl
from jax.experimental.pallas import tpu as pltpu
from jax.sharding import PartitionSpec as P

GROUP = 16
CHUNK = 8
LIST = 8
STATIC = 24
LATE_GROUP = 16
UNROLL = True
DIRECT = 2
SPAN = 4096
NOTHING = 2048
ROWS = 16
VMEM_LIMIT = 12 * 1024 * 1024


def far_rows(far, row, tiles):
    ntr = far.shape[0] // tiles
    keep = jnp.where(row < tiles, 1.0, 0.0).astype(jnp.float32)
    x = far[pl.ds(jnp.where(row < tiles, row, 0), ntr, stride=tiles), :] * keep
    x = jnp.concatenate([x, jnp.zeros((ROWS - ntr, 128), jnp.float32)], axis=0)
    high = x.astype(jnp.bfloat16)
    low = (x - high.astype(jnp.float32)).astype(jnp.bfloat16)
    return jnp.concatenate([high, low], axis=0)


def dot_nt(x, t):
    return lax.dot_general(x, t, (((1,), (1,)), ((), ())), preferred_element_type=jnp.float32)


def split_rows(field, row, tiles):
    x = field[pl.ds(row, ROWS, stride=tiles), :]
    high = x.astype(jnp.bfloat16)
    low = (x - high.astype(jnp.float32)).astype(jnp.bfloat16)
    return jnp.concatenate([high, low], axis=0)


def copy_rows(refs, field, sem):
    copies, row = [], 0
    for i, ref in enumerate(refs):
        copies.append(pltpu.make_async_copy(ref, field.at[pl.ds(row, ref.shape[0])], sem.at[i]))
        row += ref.shape[0]
    for copy in copies:
        copy.start()
    return copies


def block_copy(transport, which, blocks, sem, c):
    at = pl.ds(c * CHUNK, CHUNK)
    return pltpu.make_async_copy(transport.at[which, at], blocks.at[at], sem.at[c])


def split_index(index, size):
    if size & (size - 1) == 0:
        high = lax.shift_right_logical(index, jnp.int32(size.bit_length() - 1))
    else:
        high = lax.div(index, jnp.int32(size))
    return high, index - high * size


def table_rows(nb, col_blocks):
    order_row = 2 * nb
    list_row = order_row + col_blocks
    return order_row, list_row, list_row + nb


def index_table(tiles, nb, ntr, regions, picks, staged):
    here = lax.axis_index("region")
    odd = lax.rem(here, 2)
    near = here + 1 - 2 * odd
    far = lax.rem(here + 2 * odd - 1 + regions, regions)
    rows = ntr * tiles
    staged[...] = jnp.zeros_like(staged)
    chosen = [jnp.full((1, tiles), NOTHING, jnp.int32) for _ in range(nb)]
    used = jnp.zeros((1, tiles), jnp.int32)
    for b in range(nb):
        p = picks[b:b + 1, :]
        in_here = (p >= here * tiles) & (p < (here + 1) * tiles)
        in_near = (p >= near * tiles) & (p < (near + 1) * tiles)
        distant = jnp.where(in_here | in_near, 0, 1)
        away = p - far * tiles
        staged[b:b + 1, :] = jnp.where(in_here, p - here * tiles, jnp.where(in_near, p - near * tiles + rows, 2 * rows))
        for m in range(b + 1):
            chosen[m] = jnp.where((distant == 1) & (used == m), away + b * SPAN, chosen[m])
        used = used + distant
    for m in range(nb):
        staged[nb + m:nb + m + 1, :] = chosen[m]
    return here


def early_products(tiles, nb, col_blocks, table, field, blocks, partial, ready):
    order_row, list_row, count_row = table_rows(nb, col_blocks)

    def put(n, e):
        row, lane = split_index(n, tiles)
        table[list_row + row, lane] = e

    def step(c, n):
        ready(c)
        for u in range(GROUP):
            t = c * GROUP + u
            xs = [split_rows(field, table[b, t], tiles) for b in range(nb)]
            for m in range(DIRECT, nb):
                e = table[nb + m, t]
                put(n, t * (nb * SPAN) + e)
                n = n + jnp.where(e == NOTHING, 0, 1).astype(jnp.int32)
            r = dot_nt(jnp.concatenate(xs, axis=1), jnp.concatenate([blocks[t, b] for b in range(nb)], axis=1))
            partial[t] = r[:ROWS] + r[ROWS:]
        return n

    n = lax.fori_loop(0, tiles // GROUP, step, jnp.int32(0))
    table[count_row, 0] = n
    for i in range(STATIC):
        put(n + i, NOTHING)


def early_first_kernel(tiles, nb, ntr, col_blocks, regions, picks_in, own, near, transport, blocks, partial, table,
                       picks, staged, field, psem, fsem, bsem):
    index = pltpu.make_async_copy(picks_in.at[0], picks, psem)
    index.start()
    copies = copy_rows((own, near), field, fsem)
    for c in range(tiles // CHUNK):
        block_copy(transport, 0, blocks, bsem, c).start()
    rows = ntr * tiles
    field[2 * rows:, :] = jnp.zeros((field.shape[0] - 2 * rows, 128), jnp.float32)
    index.wait()
    index_table(tiles, nb, ntr, regions, picks, staged)
    index = pltpu.make_async_copy(staged, table, psem)
    index.start()
    for copy in copies:
        copy.wait()
    index.wait()

    def ready(c):
        for i in range(GROUP // CHUNK):
            block_copy(transport, 0, blocks, bsem, c * (GROUP // CHUNK) + i).wait()

    early_products(tiles, nb, col_blocks, table, field, blocks, partial, ready)


def early_second_kernel(tiles, nb, ntr, col_blocks, regions, picks_in, order_in, rates_in, coupling_in, sinking,
                        own, near, near_end, transport, blocks, partial, table, level_rates, mix, sink,
                        picks, staged, field, order, rates, coupling, psem, fsem, ssem, bsem):
    index = pltpu.make_async_copy(picks_in.at[1], picks, psem)
    index.start()
    small = [pltpu.make_async_copy(src, dst, ssem.at[i]) for i, (src, dst) in enumerate(
        ((order_in, order), (rates_in, rates), (coupling_in, coupling)))]
    for copy in small:
        copy.start()
    copies = copy_rows((own, near, near_end), field, fsem)
    for c in range(tiles // CHUNK):
        block_copy(transport, 1, blocks, bsem, c).start()
    rows = ntr * tiles
    field[2 * rows:, :] = jnp.zeros((field.shape[0] - 2 * rows, 128), jnp.float32)
    index.wait()
    for copy in small:
        copy.wait()
    here = index_table(tiles, nb, ntr, regions, picks, staged)
    order_row = table_rows(nb, col_blocks)[0]
    staged[order_row:order_row + col_blocks, 0:order.shape[1]] = order[...] - here * tiles
    index = pltpu.make_async_copy(staged, table, psem)
    index.start()
    for q in range(col_blocks):
        level_rates[:, q, :] = rates[:, q * 128:(q + 1) * 128]
    mix[...] = jnp.zeros_like(mix)
    sink[...] = jnp.zeros_like(sink)
    for s in range(ntr):
        mix[s, 0:ntr, :] = jnp.broadcast_to(coupling[:, s:s + 1], (ntr, 128))
        sink[s:s + 1, :] = jnp.full((1, 128), sinking[s], jnp.float32)
    for copy in copies:
        copy.wait()
    index.wait()

    def ready(c):
        for i in range(GROUP // CHUNK):
            block_copy(transport, 1, blocks, bsem, c * (GROUP // CHUNK) + i).wait()

    early_products(tiles, nb, col_blocks, table, field, blocks, partial, ready)


def place(e):
    return split_index(e, SPAN)


def far_product(tiles, nb, table, field, blocks, t):
    xs, ts = [], []
    for m in range(DIRECT):
        b, row = place(table[nb + m, t])
        xs.append(far_rows(field, row, tiles))
        ts.append(blocks[t, b])
    r = dot_nt(jnp.concatenate(xs, axis=1), jnp.concatenate(ts, axis=1))
    return r[:ROWS] + r[ROWS:]


def load_far(tiles, nb, col_blocks, table, field, blocks, total):
    order_row, list_row, count_row = table_rows(nb, col_blocks)
    total[...] = jnp.zeros_like(total)

    def rest(first, size):
        found = []
        blank = jnp.zeros((2 * ROWS, 128), jnp.bfloat16)
        for u in range(0, size, 2):
            where, xs, ts = [], [], []
            for v in range(2):
                at, lane = split_index(first + u + v, tiles)
                block, row = place(table[list_row + at, lane])
                t, b = split_index(block, nb)
                where.append(t)
                xs.append(far_rows(field, row, tiles))
                ts.append(blocks[t, b])
            x = jnp.concatenate([jnp.concatenate([xs[0], blank], axis=1), jnp.concatenate([blank, xs[1]], axis=1)], axis=0)
            r = dot_nt(x, jnp.concatenate(ts, axis=1))
            for v in range(2):
                part = r[2 * ROWS * v:2 * ROWS * (v + 1)]
                found.append((where[v], part[:ROWS] + part[ROWS:]))
        for t, r in found:
            total[t] += r

    def more(i, _):
        rest(STATIC + i * LIST, LIST)
        return 0

    lax.fori_loop(0, lax.div(jnp.maximum(table[count_row, 0] - STATIC, 0) + LIST - 1, LIST), more, 0)
    rest(jnp.int32(0), STATIC)


def late_first_kernel(tiles, nb, ntr, col_blocks, table, field, partial, blocks, out, total):
    load_far(tiles, nb, col_blocks, table, field, blocks, total)
    for t in range(tiles):
        v = far_product(tiles, nb, table, field, blocks, t) + partial[t] + total[t]
        out[pl.ds(t, ntr, stride=tiles), :] = v[:ntr]


def late_second_kernel(tiles, nb, ntr, col_blocks, table, field, partial, blocks, rates, depths, mix, sink,
                       out, total, value):
    load_far(tiles, nb, col_blocks, table, field, blocks, total)
    order_row = table_rows(nb, col_blocks)[0]
    per = LATE_GROUP // col_blocks
    steps = tiles // LATE_GROUP

    def products(c):
        for u in range(LATE_GROUP):
            t = table[order_row + u % col_blocks, c * per + u // col_blocks]
            value[c % 2 if isinstance(c, int) else lax.rem(c, 2), u] = (
                far_product(tiles, nb, table, field, blocks, t) + partial[t] + total[t])

    def chain(c, carry):
        carry = list(carry)
        for l in range(per):
            k = c * per + l
            for q in range(col_blocks):
                u = l * col_blocks + q
                t = table[order_row + q, k]
                v = value[c % 2 if isinstance(c, int) else lax.rem(c, 2), u]
                mixed = mix[0] * v[0:1]
                for s in range(1, ntr):
                    mixed = mixed + mix[s] * v[s:s + 1]
                wet = k < depths[:, q * 128:(q + 1) * 128]
                y = jnp.where(wet, v + rates[k, q:q + 1] * mixed + carry[q], jnp.float32(0.0))
                carry[q] = sink[...] * y
                out[pl.ds(t, ntr, stride=tiles), :] = y[:ntr]
        return tuple(carry)

    carry = tuple(jnp.zeros((ROWS, 128), jnp.float32) for _ in range(col_blocks))
    products(0)

    def step(c, carry):
        products(c)
        return chain(c - 1, carry)

    if UNROLL:
        for c in range(1, steps):
            carry = step(c, carry)
    else:
        carry = lax.fori_loop(1, steps, step, carry)
    chain(steps - 1, carry)


def in_hbm(x):
    return pltpu.with_memory_space_constraint(x, pltpu.HBM)


def exchange(rows):
    n = lax.axis_size("region")
    near = [(i, i ^ 1) for i in range(n)]
    far = [(i, (i + 1) % n if i % 2 else (i - 1) % n) for i in range(n)]
    b = lax.ppermute(rows, "region", far)
    a = lax.ppermute(rows, "region", near)
    return a, b


def exchange_split(rows):
    n = lax.axis_size("region")
    near = [(i, i ^ 1) for i in range(n)]
    far = [(i, (i + 1) % n if i % 2 else (i - 1) % n) for i in range(n)]
    b = lax.ppermute(rows, "region", far)
    half = rows.shape[0] // 2
    a = [lax.ppermute(rows[i * half:(i + 1) * half], "region", near) for i in range(2)]
    return a, b


def shards(tangent, transport, block_column, cell_order, depths, rates, coupling, sinking):
    tiles, ntr, cells = tangent.shape
    nb = block_column.shape[2]
    levels, col_blocks = cell_order.shape
    rows = ntr * tiles
    chunks = tiles // CHUNK
    planar = jnp.transpose(tangent, (1, 0, 2)).reshape(rows, cells)
    near, far = exchange(planar)

    smem = pl.BlockSpec(memory_space=pltpu.SMEM)
    vmem = pl.BlockSpec(memory_space=pltpu.VMEM)
    anyw = pl.BlockSpec(memory_space=pl.ANY)
    params = pltpu.CompilerParams(vmem_limit_bytes=VMEM_LIMIT)
    cost = pl.CostEstimate(
        flops=4 * tiles * nb * cells * cells * ntr, bytes_accessed=transport.size, transcendentals=0
    )
    none = pl.CostEstimate(flops=0, bytes_accessed=0, transcendentals=0)
    f32, i32 = jnp.float32, jnp.int32
    array = jax.ShapeDtypeStruct
    blocks_shape = pltpu.VMEM(transport.shape[1:], transport.dtype)
    pad = (ROWS - ntr) * tiles
    sems = pltpu.SemaphoreType.DMA

    picks = in_hbm(jnp.transpose(block_column, (0, 2, 1)))
    own = in_hbm(planar)
    table_shape = array((table_rows(nb, col_blocks)[2] + 8 & ~7, tiles), i32)
    regions = lax.axis_size("region")
    partial_shape = array((tiles, ROWS, cells), f32)
    picks_scratch = pltpu.VMEM((nb, tiles), i32)
    staged = pltpu.VMEM(table_shape.shape, i32)
    field = pltpu.VMEM((3 * rows + pad, cells), f32)
    total = pltpu.VMEM((tiles, ROWS, cells), f32)

    blocks, partial, table = pl.pallas_call(
        functools.partial(early_first_kernel, tiles, nb, ntr, col_blocks, regions),
        out_shape=(blocks_shape, partial_shape, table_shape),
        in_specs=[anyw] * 4,
        out_specs=[vmem, vmem, smem],
        scratch_shapes=[picks_scratch, staged, field, sems, sems((2,)), sems((chunks,))],
        compiler_params=params,
        cost_estimate=none,
        name="step_one_early",
    )(picks, own, near, transport)

    middle = pl.pallas_call(
        functools.partial(late_first_kernel, tiles, nb, ntr, col_blocks),
        out_shape=array((rows, cells), f32),
        in_specs=[smem, vmem, vmem, vmem],
        out_specs=vmem,
        scratch_shapes=[total],
        compiler_params=params,
        cost_estimate=cost,
        name="step_one_late",
    )(table, far, partial, blocks)

    near, far = exchange_split(middle)
    blocks, partial, table, level_rates, mix, sink = pl.pallas_call(
        functools.partial(early_second_kernel, tiles, nb, ntr, col_blocks, regions),
        out_shape=(
            blocks_shape,
            partial_shape,
            table_shape,
            array((levels, col_blocks, cells), f32),
            array((ntr, ROWS, cells), f32),
            array((ROWS, cells), f32),
        ),
        in_specs=[anyw] * 4 + [smem] + [anyw] * 4,
        out_specs=[vmem, vmem, smem, vmem, vmem, vmem],
        scratch_shapes=[
            picks_scratch,
            staged,
            field,
            pltpu.VMEM((col_blocks, levels), i32),
            pltpu.VMEM(rates.shape, f32),
            pltpu.VMEM(coupling.shape, f32),
            sems,
            sems((3,)),
            sems((3,)),
            sems((chunks,)),
        ],
        compiler_params=params,
        cost_estimate=none,
        name="step_two_early",
    )(picks, in_hbm(cell_order.T), in_hbm(rates), in_hbm(coupling), sinking, middle, *near, transport)

    result = pl.pallas_call(
        functools.partial(late_second_kernel, tiles, nb, ntr, col_blocks),
        out_shape=array((rows, cells), f32),
        in_specs=[smem, vmem] + [vmem] * 6,
        out_specs=vmem,
        scratch_shapes=[total, pltpu.VMEM((2, LATE_GROUP, ROWS, cells), f32)],
        compiler_params=params,
        cost_estimate=cost,
        name="step_two_late",
    )(table, far, partial, blocks, level_rates, depths.reshape(1, -1), mix, sink)
    return jnp.transpose(result.reshape(ntr, tiles, cells), (1, 0, 2))


def solution(mesh):
    in_specs = (
        P(("groups", "region"), None, None),
        P(None, "region", None, None, None),
        P(None, "region", None),
        P(None, "region"),
        P("region"),
        P(None, "region"),
        P(),
        P(),
    )
    out_specs = P(("groups", "region"), None, None)
    return jax.shard_map(shards, mesh=mesh, in_specs=in_specs, out_specs=out_specs, check_vma=False)
```

```python
import functools

import jax
import jax.numpy as jnp
from jax import lax
from jax.experimental import pallas as pl
from jax.experimental.pallas import tpu as pltpu
from jax.sharding import PartitionSpec as P

GROUP = 8
CHUNK = 8
LIST = 8
STATIC = 24
LATE_GROUP = 16
UNROLL = True
DIRECT = 2
SPAN = 4096
NOTHING = 2048
ROWS = 16
VMEM_LIMIT = 12 * 1024 * 1024


def far_rows(far, row, tiles):
    ntr = far.shape[0] // tiles
    keep = jnp.where(row < tiles, 1.0, 0.0).astype(jnp.float32)
    x = far[pl.ds(jnp.where(row < tiles, row, 0), ntr, stride=tiles), :] * keep
    x = jnp.concatenate([x, jnp.zeros((ROWS - ntr, 128), jnp.float32)], axis=0)
    high = x.astype(jnp.bfloat16)
    low = (x - high.astype(jnp.float32)).astype(jnp.bfloat16)
    return jnp.concatenate([high, low], axis=0)


def dot_nt(x, t):
    return lax.dot_general(x, t, (((1,), (1,)), ((), ())), preferred_element_type=jnp.float32)


def split_rows(field, row, tiles):
    x = field[pl.ds(row, ROWS, stride=tiles), :]
    high = x.astype(jnp.bfloat16)
    low = (x - high.astype(jnp.float32)).astype(jnp.bfloat16)
    return jnp.concatenate([high, low], axis=0)


def copy_rows(refs, field, sem):
    copies, row = [], 0
    for i, ref in enumerate(refs):
        copies.append(pltpu.make_async_copy(ref, field.at[pl.ds(row, ref.shape[0])], sem.at[i]))
        row += ref.shape[0]
    for copy in copies:
        copy.start()
    return copies


def block_copy(transport, which, blocks, sem, c):
    at = pl.ds(c * CHUNK, CHUNK)
    return pltpu.make_async_copy(transport.at[which, at], blocks.at[at], sem.at[c])


def split_index(index, size):
    if size & (size - 1) == 0:
        high = lax.shift_right_logical(index, jnp.int32(size.bit_length() - 1))
    else:
        high = lax.div(index, jnp.int32(size))
    return high, index - high * size


def table_rows(nb, col_blocks):
    order_row = 2 * nb
    list_row = order_row + col_blocks
    return order_row, list_row, list_row + nb


def index_table(tiles, nb, ntr, regions, picks, staged):
    here = lax.axis_index("region")
    odd = lax.rem(here, 2)
    near = here + 1 - 2 * odd
    far = lax.rem(here + 2 * odd - 1 + regions, regions)
    rows = ntr * tiles
    staged[...] = jnp.zeros_like(staged)
    chosen = [jnp.full((1, tiles), NOTHING, jnp.int32) for _ in range(nb)]
    used = jnp.zeros((1, tiles), jnp.int32)
    for b in range(nb):
        p = picks[b:b + 1, :]
        in_here = (p >= here * tiles) & (p < (here + 1) * tiles)
        in_near = (p >= near * tiles) & (p < (near + 1) * tiles)
        distant = jnp.where(in_here | in_near, 0, 1)
        away = p - far * tiles
        staged[b:b + 1, :] = jnp.where(in_here, p - here * tiles, jnp.where(in_near, p - near * tiles + rows, 2 * rows))
        for m in range(b + 1):
            chosen[m] = jnp.where((distant == 1) & (used == m), away + b * SPAN, chosen[m])
        used = used + distant
    for m in range(nb):
        staged[nb + m:nb + m + 1, :] = chosen[m]
    return here


def early_products(tiles, nb, col_blocks, table, field, blocks, partial, ready):
    order_row, list_row, count_row = table_rows(nb, col_blocks)

    def put(n, e):
        row, lane = split_index(n, tiles)
        table[list_row + row, lane] = e

    def step(c, n):
        ready(c)
        for u in range(GROUP):
            t = c * GROUP + u
            xs = [split_rows(field, table[b, t], tiles) for b in range(nb)]
            for m in range(DIRECT, nb):
                e = table[nb + m, t]
                put(n, t * (nb * SPAN) + e)
                n = n + jnp.where(e == NOTHING, 0, 1).astype(jnp.int32)
            r = dot_nt(jnp.concatenate(xs, axis=1), jnp.concatenate([blocks[t, b] for b in range(nb)], axis=1))
            partial[t] = r[:ROWS] + r[ROWS:]
        return n

    n = lax.fori_loop(0, tiles // GROUP, step, jnp.int32(0))
    table[count_row, 0] = n
    for i in range(STATIC):
        put(n + i, NOTHING)


def early_first_kernel(tiles, nb, ntr, col_blocks, regions, picks_in, own, near, transport, blocks, partial, table,
                       picks, staged, field, psem, fsem, bsem):
    index = pltpu.make_async_copy(picks_in.at[0], picks, psem)
    index.start()
    copies = copy_rows((own, near), field, fsem)
    for c in range(tiles // CHUNK):
        block_copy(transport, 0, blocks, bsem, c).start()
    rows = ntr * tiles
    field[2 * rows:, :] = jnp.zeros((field.shape[0] - 2 * rows, 128), jnp.float32)
    index.wait()
    index_table(tiles, nb, ntr, regions, picks, staged)
    index = pltpu.make_async_copy(staged, table, psem)
    index.start()
    for copy in copies:
        copy.wait()
    index.wait()

    def ready(c):
        for i in range(GROUP // CHUNK):
            block_copy(transport, 0, blocks, bsem, c * (GROUP // CHUNK) + i).wait()

    early_products(tiles, nb, col_blocks, table, field, blocks, partial, ready)


def early_second_kernel(tiles, nb, ntr, col_blocks, regions, picks_in, order_in, rates_in, coupling_in, sinking,
                        own, near, near_end, transport, blocks, partial, table, level_rates, mix, sink,
                        picks, staged, field, order, rates, coupling, psem, fsem, ssem, bsem):
    index = pltpu.make_async_copy(picks_in.at[1], picks, psem)
    index.start()
    small = [pltpu.make_async_copy(src, dst, ssem.at[i]) for i, (src, dst) in enumerate(
        ((order_in, order), (rates_in, rates), (coupling_in, coupling)))]
    for copy in small:
        copy.start()
    copies = copy_rows((own, near, near_end), field, fsem)
    for c in range(tiles // CHUNK):
        block_copy(transport, 1, blocks, bsem, c).start()
    rows = ntr * tiles
    field[2 * rows:, :] = jnp.zeros((field.shape[0] - 2 * rows, 128), jnp.float32)
    index.wait()
    for copy in small:
        copy.wait()
    here = index_table(tiles, nb, ntr, regions, picks, staged)
    order_row = table_rows(nb, col_blocks)[0]
    staged[order_row:order_row + col_blocks, 0:order.shape[1]] = order[...] - here * tiles
    index = pltpu.make_async_copy(staged, table, psem)
    index.start()
    for q in range(col_blocks):
        level_rates[:, q, :] = rates[:, q * 128:(q + 1) * 128]
    mix[...] = jnp.zeros_like(mix)
    sink[...] = jnp.zeros_like(sink)
    for s in range(ntr):
        mix[s, 0:ntr, :] = jnp.broadcast_to(coupling[:, s:s + 1], (ntr, 128))
        sink[s:s + 1, :] = jnp.full((1, 128), sinking[s], jnp.float32)
    for copy in copies:
        copy.wait()
    index.wait()

    def ready(c):
        for i in range(GROUP // CHUNK):
            block_copy(transport, 1, blocks, bsem, c * (GROUP // CHUNK) + i).wait()

    early_products(tiles, nb, col_blocks, table, field, blocks, partial, ready)


def place(e):
    return split_index(e, SPAN)


def far_product(tiles, nb, table, field, blocks, t):
    xs, ts = [], []
    for m in range(DIRECT):
        b, row = place(table[nb + m, t])
        xs.append(far_rows(field, row, tiles))
        ts.append(blocks[t, b])
    r = dot_nt(jnp.concatenate(xs, axis=1), jnp.concatenate(ts, axis=1))
    return r[:ROWS] + r[ROWS:]


def load_far(tiles, nb, col_blocks, table, field, blocks, total):
    order_row, list_row, count_row = table_rows(nb, col_blocks)
    total[...] = jnp.zeros_like(total)

    def rest(first, size):
        found = []
        blank = jnp.zeros((2 * ROWS, 128), jnp.bfloat16)
        for u in range(0, size, 2):
            where, xs, ts = [], [], []
            for v in range(2):
                at, lane = split_index(first + u + v, tiles)
                block, row = place(table[list_row + at, lane])
                t, b = split_index(block, nb)
                where.append(t)
                xs.append(far_rows(field, row, tiles))
                ts.append(blocks[t, b])
            x = jnp.concatenate([jnp.concatenate([xs[0], blank], axis=1), jnp.concatenate([blank, xs[1]], axis=1)], axis=0)
            r = dot_nt(x, jnp.concatenate(ts, axis=1))
            for v in range(2):
                part = r[2 * ROWS * v:2 * ROWS * (v + 1)]
                found.append((where[v], part[:ROWS] + part[ROWS:]))
        for t, r in found:
            total[t] += r

    def more(i, _):
        rest(STATIC + i * LIST, LIST)
        return 0

    lax.fori_loop(0, lax.div(jnp.maximum(table[count_row, 0] - STATIC, 0) + LIST - 1, LIST), more, 0)
    rest(jnp.int32(0), STATIC)


def late_first_kernel(tiles, nb, ntr, col_blocks, table, field, partial, blocks, out, total):
    load_far(tiles, nb, col_blocks, table, field, blocks, total)
    for t in range(tiles):
        v = far_product(tiles, nb, table, field, blocks, t) + partial[t] + total[t]
        out[pl.ds(t, ntr, stride=tiles), :] = v[:ntr]


def late_second_kernel(tiles, nb, ntr, col_blocks, table, field, partial, blocks, rates, depths, mix, sink,
                       out, total, value):
    load_far(tiles, nb, col_blocks, table, field, blocks, total)
    order_row = table_rows(nb, col_blocks)[0]
    per = LATE_GROUP // col_blocks
    steps = tiles // LATE_GROUP

    def products(c):
        for u in range(LATE_GROUP):
            t = table[order_row + u % col_blocks, c * per + u // col_blocks]
            value[c % 2 if isinstance(c, int) else lax.rem(c, 2), u] = (
                far_product(tiles, nb, table, field, blocks, t) + partial[t] + total[t])

    def chain(c, carry):
        carry = list(carry)
        for l in range(per):
            k = c * per + l
            for q in range(col_blocks):
                u = l * col_blocks + q
                t = table[order_row + q, k]
                v = value[c % 2 if isinstance(c, int) else lax.rem(c, 2), u]
                mixed = mix[0] * v[0:1]
                for s in range(1, ntr):
                    mixed = mixed + mix[s] * v[s:s + 1]
                wet = k < depths[:, q * 128:(q + 1) * 128]
                y = jnp.where(wet, v + rates[k, q:q + 1] * mixed + carry[q], jnp.float32(0.0))
                carry[q] = sink[...] * y
                out[pl.ds(t, ntr, stride=tiles), :] = y[:ntr]
        return tuple(carry)

    carry = tuple(jnp.zeros((ROWS, 128), jnp.float32) for _ in range(col_blocks))
    products(0)

    def step(c, carry):
        products(c)
        return chain(c - 1, carry)

    if UNROLL:
        for c in range(1, steps):
            carry = step(c, carry)
    else:
        carry = lax.fori_loop(1, steps, step, carry)
    chain(steps - 1, carry)


def in_hbm(x):
    return pltpu.with_memory_space_constraint(x, pltpu.HBM)


def exchange(rows):
    n = lax.axis_size("region")
    near = [(i, i ^ 1) for i in range(n)]
    far = [(i, (i + 1) % n if i % 2 else (i - 1) % n) for i in range(n)]
    b = lax.ppermute(rows, "region", far)
    a = lax.ppermute(rows, "region", near)
    return a, b


def exchange_split(rows):
    n = lax.axis_size("region")
    near = [(i, i ^ 1) for i in range(n)]
    far = [(i, (i + 1) % n if i % 2 else (i - 1) % n) for i in range(n)]
    b = lax.ppermute(rows, "region", far)
    half = rows.shape[0] // 2
    a = [lax.ppermute(rows[i * half:(i + 1) * half], "region", near) for i in range(2)]
    return a, b


def shards(tangent, transport, block_column, cell_order, depths, rates, coupling, sinking):
    tiles, ntr, cells = tangent.shape
    nb = block_column.shape[2]
    levels, col_blocks = cell_order.shape
    rows = ntr * tiles
    chunks = tiles // CHUNK
    planar = jnp.transpose(tangent, (1, 0, 2)).reshape(rows, cells)
    near, far = exchange(planar)

    smem = pl.BlockSpec(memory_space=pltpu.SMEM)
    vmem = pl.BlockSpec(memory_space=pltpu.VMEM)
    anyw = pl.BlockSpec(memory_space=pl.ANY)
    params = pltpu.CompilerParams(vmem_limit_bytes=VMEM_LIMIT)
    cost = pl.CostEstimate(
        flops=4 * tiles * nb * cells * cells * ntr, bytes_accessed=transport.size, transcendentals=0
    )
    none = pl.CostEstimate(flops=0, bytes_accessed=0, transcendentals=0)
    f32, i32 = jnp.float32, jnp.int32
    array = jax.ShapeDtypeStruct
    blocks_shape = pltpu.VMEM(transport.shape[1:], transport.dtype)
    pad = (ROWS - ntr) * tiles
    sems = pltpu.SemaphoreType.DMA

    picks = in_hbm(jnp.transpose(block_column, (0, 2, 1)))
    own = in_hbm(planar)
    table_shape = array((table_rows(nb, col_blocks)[2] + 8 & ~7, tiles), i32)
    regions = lax.axis_size("region")
    partial_shape = array((tiles, ROWS, cells), f32)
    picks_scratch = pltpu.VMEM((nb, tiles), i32)
    staged = pltpu.VMEM(table_shape.shape, i32)
    field = pltpu.VMEM((3 * rows + pad, cells), f32)
    total = pltpu.VMEM((tiles, ROWS, cells), f32)

    blocks, partial, table = pl.pallas_call(
        functools.partial(early_first_kernel, tiles, nb, ntr, col_blocks, regions),
        out_shape=(blocks_shape, partial_shape, table_shape),
        in_specs=[anyw] * 4,
        out_specs=[vmem, vmem, smem],
        scratch_shapes=[picks_scratch, staged, field, sems, sems((2,)), sems((chunks,))],
        compiler_params=params,
        cost_estimate=none,
        name="step_one_early",
    )(picks, own, near, transport)

    middle = pl.pallas_call(
        functools.partial(late_first_kernel, tiles, nb, ntr, col_blocks),
        out_shape=array((rows, cells), f32),
        in_specs=[smem, vmem, vmem, vmem],
        out_specs=vmem,
        scratch_shapes=[total],
        compiler_params=params,
        cost_estimate=cost,
        name="step_one_late",
    )(table, far, partial, blocks)

    near, far = exchange_split(middle)
    blocks, partial, table, level_rates, mix, sink = pl.pallas_call(
        functools.partial(early_second_kernel, tiles, nb, ntr, col_blocks, regions),
        out_shape=(
            blocks_shape,
            partial_shape,
            table_shape,
            array((levels, col_blocks, cells), f32),
            array((ntr, ROWS, cells), f32),
            array((ROWS, cells), f32),
        ),
        in_specs=[anyw] * 4 + [smem] + [anyw] * 4,
        out_specs=[vmem, vmem, smem, vmem, vmem, vmem],
        scratch_shapes=[
            picks_scratch,
            staged,
            field,
            pltpu.VMEM((col_blocks, levels), i32),
            pltpu.VMEM(rates.shape, f32),
            pltpu.VMEM(coupling.shape, f32),
            sems,
            sems((3,)),
            sems((3,)),
            sems((chunks,)),
        ],
        compiler_params=params,
        cost_estimate=none,
        name="step_two_early",
    )(picks, in_hbm(cell_order.T), in_hbm(rates), in_hbm(coupling), sinking, middle, *near, transport)

    result = pl.pallas_call(
        functools.partial(late_second_kernel, tiles, nb, ntr, col_blocks),
        out_shape=array((rows, cells), f32),
        in_specs=[smem, vmem] + [vmem] * 6,
        out_specs=vmem,
        scratch_shapes=[total, pltpu.VMEM((2, LATE_GROUP, ROWS, cells), f32)],
        compiler_params=params,
        cost_estimate=cost,
        name="step_two_late",
    )(table, far, partial, blocks, level_rates, depths.reshape(1, -1), mix, sink)
    return jnp.transpose(result.reshape(ntr, tiles, cells), (1, 0, 2))


def solution(mesh):
    in_specs = (
        P(("groups", "region"), None, None),
        P(None, "region", None, None, None),
        P(None, "region", None),
        P(None, "region"),
        P("region"),
        P(None, "region"),
        P(),
        P(),
    )
    out_specs = P(("groups", "region"), None, None)
    return jax.shard_map(shards, mesh=mesh, in_specs=in_specs, out_specs=out_specs, check_vma=False)
```
